32 devices in a mesh: ctx: 8 (over y, x, core), exp: 4 (over z).
Axes of the slice: x: 2, y: 2, z: 4, core: 2. Of those that a mesh axis runs over, the one named last changes fastest.
Arguments:
- residual: bfloat16 [1536, 2048], P('ctx', 'exp'), may hold values from -40 to 40
- queries: bfloat16 [1536, 2048], P('ctx', 'exp'), may hold values from -32 to 32
- keys: bfloat16 [1536, 2048], P('ctx', 'exp'), may hold values from -8 to 8
- values: bfloat16 [1536, 2048], P('ctx', 'exp'), may hold values from -6 to 6
- w_out: bfloat16 [2048, 2048], P('exp'), may hold values from -0.1875 to 0.1875
- moe_gain: float32 [2048], replicated, may hold values from 0.1 to 1.9
- expert_ids: int32 [1536, 8], P('ctx'), may hold values from 0 to 63, all different within a row; in each aligned block of 192 rows (0 to 191, 192 to 383, ...) at most 36 rows name the same one
- gate_weights: float32 [1536, 8], P('ctx'), may hold values from 0.05 to 0.5
- w_gate: bfloat16 [64, 2048, 1024], P('ctx', None, 'exp'), may hold values from -1 to 1
- w_up: bfloat16 [64, 2048, 1024], P('ctx', None, 'exp'), may hold values from -1 to 1
- w_down: bfloat16 [64, 1024, 2048], P('ctx', None, 'exp'), may hold values from -0.01171875 to 0.01171875
Outputs:
- mixed: bfloat16 [1536, 2048], P('ctx', 'exp')
The draws below stay inside these ranges and needn't reach their ends.
Inputs may be any that keep to these rules, and one draw needn't show every extreme that they name: `expert_ids`: each row names 8 different experts. Within the 192 rows of one block (rows b * 192 to b * 192 + 191) no expert is named more than 36 times, and in every draw some expert is named exactly 36 times in some block.
All inputs are finite; a program needn't handle non-finite values.
Results may differ from the reference program's by a relative error of at most 0.015.
Values may be sent and summed in bfloat16 or wider, within the bound.
A program may use at most 128 MiB of HBM per device.

```python
import math
import jax
import jax.numpy as jnp
import numpy as np
from jax import lax

D = 2048
H = 16
FF = 1024
E = 64
K = 8
BLK = 192
SEQ = 1536
CAP = 36


offset_level = 0.6


noise_level = 0.6


tilt_level = 12.0


def shared_normal(key):
    return jax.random.normal(jax.random.fold_in(key, 17), (SEQ, D), jnp.float32)


def offset_signs(key):
    first_dir = jnp.where(jax.random.normal(jax.random.fold_in(key, 21), (D,), jnp.float32) > 0, 1.0, -1.0)
    second_dir = jnp.where(jax.random.normal(jax.random.fold_in(key, 22), (D,), jnp.float32) > 0, 1.0, -1.0)
    return (first_dir, second_dir)


def draw_keys(key, part):
    base_normal = shared_normal(key)
    result = jnp.clip(base_normal, -6.0, 6.0)
    return result.astype(jnp.bfloat16)


def draw_queries(key, part):
    key = jax.random.fold_in(key, 9)
    result = jnp.clip(3.0 * jax.random.normal(key, (SEQ, D), jnp.float32), -18.0, 18.0)
    return result.astype(jnp.bfloat16)


def column_ramp(low_end, high_end):
    fraction = jnp.arange(D).astype(jnp.float32) / (D - 1)
    return jnp.exp(math.log(low_end) + fraction * (math.log(high_end) - math.log(low_end)))[None, :]


def draw_residual(key, part):
    first_dir, second_dir = offset_signs(key)
    key = jax.random.fold_in(key, 3)
    col_key, row_key, main_key, sign_key = jax.random.split(key, 4)
    rough = jnp.exp(jax.random.uniform(col_key, (1, D), jnp.float32, math.log(0.7), math.log(1.4)))
    row_scale = jnp.exp(jax.random.uniform(row_key, (SEQ, 1), jnp.float32, math.log(0.5), math.log(2.0)))
    row_sign = jnp.where(jax.random.normal(sign_key, (SEQ, 1), jnp.float32) > 0, 1.0, -1.0)
    col_scale = column_ramp(0.35, 2.8) * rough
    main_part = jnp.clip(jax.random.normal(main_key, (SEQ, D), jnp.float32), -5.0, 5.0)
    shifted = offset_level * (first_dir[None, :] + row_sign * second_dir[None, :])
    return (noise_level * main_part * col_scale * row_scale + shifted).astype(jnp.bfloat16)


def draw_w_gate(key, part):
    first_dir, second_dir = offset_signs(key)
    key = jax.random.fold_in(key, 11)
    base = jnp.clip(jax.random.normal(key, (E, D, FF), jnp.float32), -6.0, 6.0) / math.sqrt(D)
    return (base + tilt_level / D * first_dir[None, :, None]).astype(jnp.bfloat16)


def draw_w_up(key, part):
    first_dir, second_dir = offset_signs(key)
    key = jax.random.fold_in(key, 13)
    noise_key, sign_key = jax.random.split(key, 2)
    base = jnp.clip(jax.random.normal(noise_key, (E, D, FF), jnp.float32), -6.0, 6.0) / math.sqrt(D)
    unit_sign = jnp.where(jax.random.normal(sign_key, (E, 1, FF), jnp.float32) > 0, 1.0, -1.0)
    return (base + tilt_level / D * second_dir[None, :, None] * unit_sign).astype(jnp.bfloat16)


def strengthened(values, key, source, target, shards_of, factor):
    def block_of(dim):
        return (jnp.arange(values.shape[dim]) // (values.shape[dim] // shards_of)).reshape((-1,) + (1,) * (values.ndim - 1 - dim))

    near = jax.random.permutation(key, shards_of)[block_of(target)]
    other_side = (block_of(target) + shards_of // 2) % shards_of
    return jnp.where((block_of(source) == near) | (block_of(source) == other_side), factor * values, values)


def shard_levels(stream_key, shape, pieces, low, high):
    level = 1.0
    for dim, shards_of in pieces:
        heights = jax.random.uniform(jax.random.fold_in(jax.random.fold_in(stream_key, 6), dim), (shards_of,), jnp.float32, low / len(pieces), high / len(pieces))
        level = level * jnp.repeat(jnp.exp(heights), shape[dim] // shards_of).reshape((-1,) + (1,) * (len(shape) - 1 - dim))
    return level


def routed_block(stream_key, own, number, rows, count, top, most, skew):
    sequence = jax.random.permutation(stream_key, count)
    heavy_load, ordinary = portions_of(count, rows * top, most, skew, True), portions_of(count, rows * top, most, skew, False)
    places = jnp.arange(count)

    def named(tallies, turn):
        used = int((tallies > 0).sum())
        fixed = max(1, used // 4)
        moved = fixed + (places - fixed + turn * (used - fixed)) % max(1, count - fixed)
        return jnp.zeros((count,), jnp.int32).at[sequence[jnp.where(places < fixed, places, moved)]].set(jnp.asarray(tallies, jnp.int32))

    tallies = jnp.where(number % 4 == 0, named(heavy_load, number // 4), named(ordinary, number - number // 4 - 1))
    mixed = jax.random.permutation(jax.random.fold_in(own, 3), count)
    donor, taker = mixed[0:count // 2 * 2:2], mixed[1:count // 2 * 2:2]
    margin = jnp.minimum(tallies[donor] - 1, most - tallies[taker]) // 2
    margin = jnp.where((donor == sequence[0]) | (taker == sequence[0]) | (tallies[taker] == 0), 0, jnp.maximum(margin, 0))
    moved = jax.random.randint(jax.random.fold_in(own, 4), (count // 2,), 0, 1 << 20) % (margin + 1)
    tallies = tallies.at[donor].add(-moved).at[taker].add(moved)
    items = jnp.searchsorted(jnp.cumsum(tallies), jnp.arange(rows * top), side="right").astype(jnp.int32)
    listing = items.reshape(top, rows).T
    listing = listing[jax.random.permutation(jax.random.fold_in(own, 1), rows)]
    turn = jax.random.randint(jax.random.fold_in(own, 2), (rows, 1), 0, top)
    return jnp.take_along_axis(listing, (jnp.arange(top)[None, :] + turn) % top, axis=1)


def portions_of(amount, total, limit, slope, full):
    weights = [(1 << 20) // math.isqrt(grade ** slope) + 1 for grade in range(1, amount + 1)]
    largest = limit if full else min(limit, max(-(-total // amount), total * weights[0] // sum(weights)))
    least = 1 if total - largest >= amount - 1 else 0
    holding, spare = [largest] + [least] * (amount - 1), total - largest - least * (amount - 1)
    while spare > 0:
        movable = [i for i in range(1, amount) if holding[i] < largest] or [i for i in range(1, amount) if holding[i] < limit]
        pool, budget = sum([weights[i] for i in movable]), spare
        for i in movable:
            extra = min(limit - holding[i], max(1, budget * weights[i] // pool), spare)
            holding[i] = holding[i] + extra
            spare = spare - extra
    return np.array(holding)


def normal_values(own_key, dims, width, reach, pieces=(), held_as=jnp.bfloat16):
    gain = shard_levels(own_key, dims, pieces, -0.22, 0.18) if pieces else 1.0
    array = jax.random.normal(own_key, dims, jnp.float32) * width * gain
    return jnp.minimum(jnp.maximum(array, -reach), reach).astype(held_as)


def heavy_noise(rng, extent, deviation, reach, cuts, heavy, held_as=jnp.bfloat16):
    array = deviation * jax.random.normal(rng, extent, jnp.float32)
    if cuts:
        array = array * shard_levels(rng, extent, cuts, -0.22, 0.18)
    return jnp.clip(strengthened(array, jax.random.fold_in(rng, 3), *heavy), -reach, reach).astype(held_as)


def setup_inputs(seed: int = 0) -> dict:
    arg_keys = jax.random.split(jax.random.key(seed), 12)
    residual = draw_residual(jax.random.fold_in(arg_keys[11], 71), 0)
    queries = draw_queries(jax.random.fold_in(arg_keys[11], 71), 0)
    keys = draw_keys(jax.random.fold_in(arg_keys[11], 71), 0)
    values = normal_values(arg_keys[3], (SEQ, D), 1.0, 6.0, ((0, 8), (1, 4)))
    w_out = heavy_noise(arg_keys[4], (D, D), D ** -0.5, 0.1875, ((0, 4),), (0, 1, 4, 2.0))
    moe_gain = jnp.clip(1.0 + 0.18 * jax.random.normal(arg_keys[5], (D,), jnp.float32), 0.1, 1.9)
    expert_ids_keys = jax.random.split(jax.random.fold_in(arg_keys[6], 1), SEQ // BLK)
    expert_ids_turns = jax.random.permutation(jax.random.fold_in(arg_keys[6], 3), SEQ // BLK)
    expert_ids = jax.vmap(lambda own, number: routed_block(jax.random.fold_in(arg_keys[6], 2), own, number, BLK, E, K, CAP, 2))(expert_ids_keys, expert_ids_turns).reshape((SEQ, K))
    gate_weights = jnp.clip(jnp.exp(math.log(0.5) - 2.3025851 * jax.random.uniform(arg_keys[7], (SEQ, K), jnp.float32) ** shard_levels(arg_keys[7], (SEQ, K), ((0, 8),), -0.2, 0.2)), 0.05, 0.5)
    w_gate = draw_w_gate(jax.random.fold_in(arg_keys[11], 71), 0)
    w_up = draw_w_up(jax.random.fold_in(arg_keys[11], 71), 0)
    w_down = normal_values(arg_keys[10], (E, FF, D), (256 * FF) ** -0.5, 0.01171875, ((0, 8), (2, 4)))
    return dict(residual=residual, queries=queries, keys=keys, values=values, w_out=w_out, moe_gain=moe_gain, expert_ids=expert_ids, gate_weights=gate_weights, w_gate=w_gate, w_up=w_up, w_down=w_down)


def reference(residual, queries, keys, values, w_out, moe_gain, expert_ids, gate_weights, w_gate, w_up, w_down):
    seq_len = residual.shape[0]
    head_dim = D // H
    score_scale = 1.0 / math.sqrt(head_dim)
    q_heads = queries.reshape(seq_len, H, head_dim).transpose(1, 0, 2)
    k_heads = keys.reshape(seq_len, H, head_dim).transpose(1, 0, 2)
    v_heads = values.reshape(seq_len, H, head_dim).transpose(1, 0, 2)
    position = jnp.arange(seq_len).astype(jnp.int32)
    causal = position[None, :] <= position[:, None]

    def one_head(operands):
        q_one, k_one, v_one = operands
        scores = jnp.dot(q_one, k_one.T, preferred_element_type=jnp.float32) * score_scale
        masked = jnp.where(causal, scores, -jnp.inf)
        row_max = lax.optimization_barrier(jnp.max(masked, axis=1, keepdims=True))
        weights = jnp.where(causal, jnp.exp(masked - row_max), 0.0)
        row_total = lax.optimization_barrier(jnp.sum(weights, axis=1, keepdims=True))
        probabilities = weights.astype(jnp.bfloat16)
        mixed_values = jnp.dot(probabilities, v_one, preferred_element_type=jnp.float32)
        return (mixed_values / row_total).astype(jnp.bfloat16)
    head_outputs = lax.map(one_head, (q_heads, k_heads, v_heads))
    attn_heads = head_outputs.transpose(1, 0, 2).reshape(seq_len, D)
    attn_sum = jnp.dot(attn_heads, w_out, preferred_element_type=jnp.float32)
    post_attn = (residual.astype(jnp.float32) + attn_sum).astype(jnp.bfloat16)
    state_wide = post_attn.astype(jnp.float32)
    mean_square = lax.optimization_barrier(jnp.mean(state_wide * state_wide, axis=1, keepdims=True))
    moe_in = (state_wide * lax.rsqrt(mean_square + 1e-05) * moe_gain).astype(jnp.bfloat16)
    block_count = seq_len // BLK
    flat_ids = expert_ids.reshape(block_count, BLK * K).astype(jnp.int32)
    onehot = (flat_ids[:, :, None] == jnp.arange(E).astype(jnp.int32)[None, None, :]).astype(jnp.int32)
    rank_in = jnp.cumsum(onehot, axis=1) - 1
    slot_of = lax.optimization_barrier(jnp.sum(rank_in * onehot, axis=2))
    place_at = (slot_of + (jnp.arange(block_count).astype(jnp.int32) * CAP)[:, None]).reshape(-1).astype(jnp.int32)
    expert_flat = flat_ids.reshape(-1)
    token_of = (jnp.arange(seq_len * K).astype(jnp.int32) // K).astype(jnp.int32)
    slot_table = jnp.full((E, block_count * CAP), -1, jnp.int32).at[expert_flat, place_at].set(token_of)

    def one_expert(operands):
        rows_index, gate_w, up_w, down_w = operands
        is_filled = (rows_index >= 0)[:, None]
        row_data = jnp.where(is_filled, moe_in[jnp.maximum(rows_index, 0)], jnp.zeros((), jnp.bfloat16))
        gate_pre = jnp.dot(row_data, gate_w, preferred_element_type=jnp.float32)
        up_pre = jnp.dot(row_data, up_w, preferred_element_type=jnp.float32)
        hidden = (jax.nn.silu(gate_pre) * up_pre).astype(jnp.bfloat16)
        return jnp.dot(hidden, down_w, preferred_element_type=jnp.float32).astype(jnp.bfloat16)
    outputs = lax.map(one_expert, (slot_table, w_gate, w_up, w_down))
    picked = outputs[expert_flat, place_at].reshape(seq_len, K, D)
    combined = jnp.einsum('tk,tkd->td', gate_weights.astype(jnp.float32), picked.astype(jnp.float32))
    return (state_wide + combined).astype(jnp.bfloat16)
```

```python
import math

import jax
import jax.numpy as jnp
from jax import lax
from jax.sharding import PartitionSpec as P

D = 2048
H = 16
K = 8
CAP = 36
GROUP = 4


epsilon = 1e-05


def attend(carried, pieces, q_three, query_pos):
    row_max, row_total, row_accum = carried
    key_piece, value_piece = pieces
    piece_rows = key_piece.shape[0]
    heads_here = q_three.shape[1]
    head_dim = q_three.shape[2]
    k_three = key_piece.reshape(piece_rows, heads_here, head_dim)
    v_three = value_piece.reshape(piece_rows, heads_here, head_dim)
    score_scale = 1.0 / math.sqrt(head_dim)
    scores = (
        jnp.einsum("qhd,khd->qhk", q_three, k_three, preferred_element_type=jnp.float32)
        * score_scale
    )
    allowed = (jnp.arange(piece_rows, dtype=jnp.int32)[None, :] <= query_pos[:, None])[:, None, :]
    masked = jnp.where(allowed, scores, -1e30)
    new_max = jnp.maximum(row_max, jnp.max(masked, axis=2))
    weights = jnp.where(allowed, jnp.exp(masked - new_max[:, :, None]), 0.0)
    row_total = jnp.sum(weights, axis=2)
    update = jnp.einsum(
        "qhk,khd->qhd", weights.astype(jnp.bfloat16), v_three, preferred_element_type=jnp.float32
    )
    row_accum = update
    return (new_max, row_total, row_accum)


def local(
    residual, queries, keys, values, w_out, moe_gain, expert_ids, gate_weights, w_gate, w_up, w_down
):
    block_rows, col_width = queries.shape
    head_dim = D // H
    heads_here = col_width // head_dim
    experts_here = w_gate.shape[0]
    columns = lax.axis_size("ctx")
    ctx_index = lax.axis_index("ctx")
    query_pos = ctx_index * block_rows + jnp.arange(block_rows, dtype=jnp.int32)
    q_three = queries.reshape(block_rows, heads_here, head_dim)
    start_state = (
        jnp.full((block_rows, heads_here), -1e30, jnp.float32),
        jnp.zeros((block_rows, heads_here), jnp.float32),
        jnp.zeros((block_rows, heads_here, head_dim), jnp.float32),
    )
    row_max, row_total, row_accum = attend(
        start_state,
        (
            lax.all_gather(keys, "ctx", axis=0, tiled=True),
            lax.all_gather(values, "ctx", axis=0, tiled=True),
        ),
        q_three,
        query_pos,
    )
    attn_heads = (
        (row_accum / row_total[:, :, None]).reshape(block_rows, col_width).astype(jnp.bfloat16)
    )
    routing = lax.all_gather(
        jnp.concatenate([expert_ids.astype(jnp.float32), gate_weights], axis=1),
        "ctx",
        axis=0,
        tiled=True,
    )
    here = (ctx_index * experts_here + jnp.arange(experts_here, dtype=jnp.int32)).astype(
        jnp.float32
    )
    match = routing[:, :K, None] == here[None, None, :]
    chosen = jnp.any(match, axis=1)
    gates = jnp.sum(jnp.where(match, routing[:, K:, None], 0.0), axis=1)
    before = jnp.tril(jnp.ones((block_rows, block_rows), jnp.bfloat16), -1)
    rank = jnp.einsum(
        "ut,btj->buj",
        before,
        chosen.astype(jnp.bfloat16).reshape(columns, block_rows, experts_here),
        preferred_element_type=jnp.float32,
    )
    groups = columns // GROUP
    offset = ((jnp.arange(columns) % GROUP) * CAP).astype(jnp.float32)[:, None, None]
    place = jnp.where(
        chosen.reshape(columns, block_rows, experts_here), rank + offset, -1.0
    ).reshape(groups, GROUP * block_rows, experts_here)
    slots = jnp.arange(GROUP * CAP, dtype=jnp.int32).astype(jnp.float32)
    place_t = place.transpose(0, 2, 1)
    pick = place_t[:, :, None, :] == slots[None, None, :, None]
    gates_t = gates.reshape(groups, GROUP * block_rows, experts_here).transpose(0, 2, 1)
    slot_gate = jnp.sum(jnp.where(pick, gates_t[:, :, None, :], 0.0), axis=3)
    pick = pick.astype(jnp.bfloat16)
    attn_cols = lax.psum_scatter(
        jnp.dot(attn_heads, w_out, preferred_element_type=jnp.float32).astype(jnp.bfloat16),
        "exp",
        scatter_dimension=1,
        tiled=True,
    ).astype(jnp.float32)
    post_cols = (residual.astype(jnp.float32) + attn_cols).astype(jnp.bfloat16)
    post_wide = lax.all_gather(post_cols, "exp", axis=1, tiled=True).astype(jnp.float32)
    mean_square = jnp.mean(post_wide * post_wide, axis=1, keepdims=True)
    moe_rows = (post_wide * lax.rsqrt(mean_square + epsilon) * moe_gain[None, :]).astype(
        jnp.bfloat16
    )
    moe_all = lax.all_gather(moe_rows, "ctx", axis=0, tiled=True)
    packed = jnp.einsum(
        "gjst,gtd->gjsd",
        pick,
        moe_all.reshape(groups, GROUP * block_rows, D),
        preferred_element_type=jnp.float32,
    ).astype(jnp.bfloat16)
    gate_pre = jnp.einsum("gjsd,jdf->gjsf", packed, w_gate, preferred_element_type=jnp.float32)
    up_pre = jnp.einsum("gjsd,jdf->gjsf", packed, w_up, preferred_element_type=jnp.float32)
    hidden = (jax.nn.silu(gate_pre) * up_pre * slot_gate[..., None]).astype(jnp.bfloat16)
    hidden_all = lax.all_gather(hidden, "exp", axis=3, tiled=True)
    expert_out = jnp.einsum(
        "gjsf,jfd->gjsd", hidden_all, w_down, preferred_element_type=jnp.float32
    ).astype(jnp.bfloat16)
    partial = jnp.einsum("gjst,gjsd->gtd", pick, expert_out, preferred_element_type=jnp.float32)
    combined = lax.psum_scatter(
        partial.reshape(columns * block_rows, col_width).astype(jnp.bfloat16),
        "ctx",
        scatter_dimension=0,
        tiled=True,
    )
    return (post_cols.astype(jnp.float32) + combined.astype(jnp.float32)).astype(jnp.bfloat16)


def solution(mesh):
    placed = (
        P("ctx", "exp"),
        P("ctx", "exp"),
        P("ctx", "exp"),
        P("ctx", "exp"),
        P("exp", None),
        P(),
        P("ctx", None),
        P("ctx", None),
        P("ctx", None, "exp"),
        P("ctx", None, "exp"),
        P("ctx", None, "exp"),
    )
    return jax.shard_map(
        local, mesh=mesh, in_specs=placed, out_specs=P("ctx", "exp"), check_vma=False
    )
```

```python
import functools
import math

import jax
import jax.numpy as jnp
from jax import lax
from jax.experimental import pallas as pl
from jax.experimental.pallas import tpu as pltpu
from jax.sharding import PartitionSpec as P

D = 2048
H = 16
K = 8
CAP = 36
GROUP = 4
LAG = 2
MESH = pl.DeviceIdType.MESH


epsilon = 1e-05


def gather_kernel(n, k_ref, v_ref, ko_ref, vo_ref, own_sem, far_send, far_recv, sib_send, sib_recv):
    me = lax.axis_index("ctx")
    core, chip, chips = lax.rem(me, 2), me // 2, n // 2
    rows = k_ref.shape[0]
    sibling = chip * 2 + 1 - core
    peers = [lax.rem(chip + d, chips) * 2 + core for d in range(1, chips)]
    barrier = pltpu.get_barrier_semaphore()
    for other in [sibling] + peers:
        pl.semaphore_signal(barrier, inc=1, device_id={"ctx": other}, device_id_type=MESH)
    pl.semaphore_wait(barrier, chips)

    def block(ref, index):
        return ref.at[pl.ds(pl.multiple_of(index * rows, rows), rows)]

    pairs = ((k_ref, ko_ref), (v_ref, vo_ref))
    far, near, own = [], [], []
    for a, (src, dst) in enumerate(pairs):
        for d, peer in enumerate(peers):
            copy = pltpu.make_async_remote_copy(
                src_ref=src,
                dst_ref=block(dst, me),
                send_sem=far_send.at[a, d],
                recv_sem=far_recv.at[a, d],
                device_id={"ctx": peer},
                device_id_type=MESH,
            )
            copy.start()
            far.append((a, d, copy))
    for a, (src, dst) in enumerate(pairs):
        copy = pltpu.make_async_remote_copy(
            src_ref=src,
            dst_ref=block(dst, me),
            send_sem=sib_send.at[a, chips - 1],
            recv_sem=sib_recv.at[a, chips - 1],
            device_id={"ctx": sibling},
            device_id_type=MESH,
        )
        copy.start()
        near.append(copy)
        copy = pltpu.make_async_copy(src, block(dst, me), own_sem.at[a])
        copy.start()
        own.append(copy)
    for a, d, copy in far:
        copy.wait_recv()
        origin = lax.rem(chip + chips - d - 1, chips) * 2 + core
        dst = pairs[a][1]
        onward = pltpu.make_async_remote_copy(
            src_ref=block(dst, origin),
            dst_ref=block(dst, origin),
            send_sem=sib_send.at[a, d],
            recv_sem=sib_recv.at[a, d],
            device_id={"ctx": sibling},
            device_id_type=MESH,
        )
        onward.start()
        near.append(onward)
    for copy in own:
        copy.wait()
    for _, _, copy in far:
        copy.wait_send()
    for copy in near:
        copy.wait()


def gather_keys_values(keys, values, n):
    rows, width = keys.shape
    full = jax.ShapeDtypeStruct((n * rows, width), keys.dtype)
    return pl.pallas_call(
        functools.partial(gather_kernel, n),
        out_shape=(full, full),
        in_specs=[pl.BlockSpec(memory_space=pl.ANY)] * 2,
        out_specs=[pl.BlockSpec(memory_space=pl.ANY)] * 2,
        scratch_shapes=[
            pltpu.SemaphoreType.DMA((2,)),
            pltpu.SemaphoreType.DMA((2, n // 2)),
            pltpu.SemaphoreType.DMA((2, n // 2)),
            pltpu.SemaphoreType.DMA((2, n // 2)),
            pltpu.SemaphoreType.DMA((2, n // 2)),
        ],
        compiler_params=pltpu.CompilerParams(collective_id=1, has_side_effects=True),
        cost_estimate=pl.CostEstimate(flops=0, bytes_accessed=60_000_000, transcendentals=0),
    )(keys, values)


def expert_kernel(n, count, x_ref, g_ref, wg_ref, wu_ref, wd_ref, out_ref, held, send, recv):
    me = lax.axis_index("exp")
    step = pl.program_id(0)
    groups, _, slots, width = x_ref.shape
    rows = groups * slots
    units = wg_ref.shape[2]
    has_left, has_right = me > 0, me < n - 1

    def hop(side, source, expert):
        return pltpu.make_async_remote_copy(
            src_ref=held.at[source, expert],
            dst_ref=held.at[source, expert],
            send_sem=send.at[side, source, expert],
            recv_sem=recv.at[source, expert],
            device_id={"exp": me + 1 if side else me - 1},
            device_id_type=MESH,
        )

    barrier = pltpu.get_barrier_semaphore()

    @pl.when(step == 0)
    def _():
        for side, there in ((0, has_left), (1, has_right)):

            @pl.when(there)
            def _():
                pl.semaphore_signal(
                    barrier,
                    inc=1,
                    device_id={"exp": me + 1 if side else me - 1},
                    device_id_type=MESH,
                )

        pl.semaphore_wait(barrier, jnp.minimum(me, 1) + jnp.minimum(n - 1 - me, 1))

    @pl.when(step < count)
    def _():
        x = x_ref[...].reshape(rows, width)
        gate = jnp.dot(x, wg_ref[0], preferred_element_type=jnp.float32)
        up = jnp.dot(x, wu_ref[0], preferred_element_type=jnp.float32)
        hidden = gate / (1.0 + jnp.exp(-gate)) * up * g_ref[0]
        held[me, step] = hidden.astype(jnp.bfloat16)
        for side, there in ((0, has_left), (1, has_right)):

            @pl.when(there)
            def _():
                hop(side, me, step).start()

    for distance in range(1, n):
        expert = step - LAG * distance
        for side in (0, 1):
            source = me + distance if side == 0 else me - distance
            onward = has_left if side == 0 else has_right
            inside = (source < n) if side == 0 else (source >= 0)

            @pl.when((expert >= 0) & (expert < count) & inside)
            def _():
                hop(side, source, expert).wait_recv()

                @pl.when(onward)
                def _():
                    hop(side, source, expert).start()

    done = step - LAG * (n - 1)

    @pl.when(done >= 0)
    def _():
        total = jnp.zeros((rows, wd_ref.shape[2]), jnp.float32)
        for source in range(n):
            total += jnp.dot(
                held[source, done],
                wd_ref[0, source * units : (source + 1) * units],
                preferred_element_type=jnp.float32,
            )
        out_ref[...] = total.astype(jnp.bfloat16).reshape(out_ref.shape)

    @pl.when(done == count - 1)
    def _():
        for source in range(n):
            for side, there in (
                (0, has_left & (me <= source)),
                (1, has_right & (me >= source)),
            ):

                @pl.when(there)
                def _():
                    @pl.loop(0, count)
                    def _(expert):
                        hop(side, source, expert).wait_send()


def run_experts(packed, slot_gate, w_gate, w_up, w_down, n):
    groups, count, slots, width = packed.shape
    rows = groups * slots
    units, hidden, columns = w_gate.shape[2], w_down.shape[1], w_down.shape[2]
    late = LAG * (n - 1)

    def first(step):
        return jnp.minimum(step, count - 1)

    def second(step):
        return jnp.maximum(step - late, 0)

    return pl.pallas_call(
        functools.partial(expert_kernel, n, count),
        grid=(count + late,),
        out_shape=jax.ShapeDtypeStruct((groups, count, slots, columns), jnp.bfloat16),
        in_specs=[
            pl.BlockSpec((groups, 1, slots, width), lambda i: (0, first(i), 0, 0)),
            pl.BlockSpec((1, rows, 1), lambda i: (first(i), 0, 0)),
            pl.BlockSpec((1, width, units), lambda i: (first(i), 0, 0)),
            pl.BlockSpec((1, width, units), lambda i: (first(i), 0, 0)),
            pl.BlockSpec((1, hidden, columns), lambda i: (second(i), 0, 0)),
        ],
        out_specs=pl.BlockSpec((groups, 1, slots, columns), lambda i: (0, second(i), 0, 0)),
        scratch_shapes=[
            pltpu.VMEM((n, count, rows, units), jnp.bfloat16),
            pltpu.SemaphoreType.DMA((2, n, count)),
            pltpu.SemaphoreType.DMA((n, count)),
        ],
        compiler_params=pltpu.CompilerParams(
            collective_id=2, has_side_effects=True, vmem_limit_bytes=40 * 1024 * 1024
        ),
        cost_estimate=pl.CostEstimate(
            flops=8_000_000_000, bytes_accessed=100_000_000, transcendentals=0
        ),
    )(packed, slot_gate, w_gate, w_up, w_down)


def scatter_kernel(n, part_ref, out_ref, near, stage, far, near_send, near_recv, send, recv):
    me = lax.axis_index("ctx")
    core, chip, chips = lax.rem(me, 2), me // 2, n // 2
    sibling = chip * 2 + 1 - core
    barrier = pltpu.get_barrier_semaphore()
    for other in [sibling] + [lax.rem(chip + d, chips) * 2 + core for d in range(1, chips)]:
        pl.semaphore_signal(barrier, inc=1, device_id={"ctx": other}, device_id_type=MESH)
    pl.semaphore_wait(barrier, chips)

    def pass_over(d):
        target = lax.rem(chip + d, chips)
        return pltpu.make_async_remote_copy(
            src_ref=part_ref.at[target * 2 + 1 - core],
            dst_ref=near.at[d],
            send_sem=near_send.at[d],
            recv_sem=near_recv.at[d],
            device_id={"ctx": sibling},
            device_id_type=MESH,
        )

    def send_off(d):
        return pltpu.make_async_remote_copy(
            src_ref=stage.at[d],
            dst_ref=far.at[d],
            send_sem=send.at[d],
            recv_sem=recv.at[d],
            device_id={"ctx": lax.rem(chip + d, chips) * 2 + core},
            device_id_type=MESH,
        )

    order = list(range(1, chips)) + [0]
    for d in order:
        pass_over(d).start()
    for d in order:
        pass_over(d).wait_recv()
        mine = part_ref[lax.rem(chip + d, chips) * 2 + core].astype(jnp.float32)
        both = mine + near[d].astype(jnp.float32)
        if d:
            stage[d] = both.astype(jnp.bfloat16)
            send_off(d).start()
        else:
            out_ref[...] = both
    for d in range(1, chips):
        send_off(d).wait_recv()
        out_ref[...] += far[d].astype(jnp.float32)
    for d in range(1, chips):
        send_off(d).wait_send()
    for d in order:
        pass_over(d).wait_send()


def scatter_sum(part, n):
    _, rows, width = part.shape
    half = pltpu.VMEM((n // 2, rows, width), jnp.bfloat16)
    sems = pltpu.SemaphoreType.DMA((n // 2,))
    return pl.pallas_call(
        functools.partial(scatter_kernel, n),
        out_shape=jax.ShapeDtypeStruct((rows, width), jnp.float32),
        in_specs=[pl.BlockSpec(memory_space=pltpu.VMEM)],
        out_specs=pl.BlockSpec(memory_space=pltpu.VMEM),
        scratch_shapes=[half, half, half, sems, sems, sems, sems],
        compiler_params=pltpu.CompilerParams(
            collective_id=3, has_side_effects=True, vmem_limit_bytes=40 * 1024 * 1024
        ),
    )(part)


def attend(carried, pieces, q_three, query_pos):
    row_max, row_total, row_accum = carried
    key_piece, value_piece = pieces
    piece_rows = key_piece.shape[0]
    heads_here = q_three.shape[1]
    head_dim = q_three.shape[2]
    k_three = key_piece.reshape(piece_rows, heads_here, head_dim)
    v_three = value_piece.reshape(piece_rows, heads_here, head_dim)
    score_scale = 1.0 / math.sqrt(head_dim)
    scores = (
        jnp.einsum("qhd,khd->qhk", q_three, k_three, preferred_element_type=jnp.float32)
        * score_scale
    )
    allowed = (jnp.arange(piece_rows, dtype=jnp.int32)[None, :] <= query_pos[:, None])[:, None, :]
    masked = jnp.where(allowed, scores, -1e30)
    new_max = jnp.maximum(row_max, jnp.max(masked, axis=2))
    weights = jnp.where(allowed, jnp.exp(masked - new_max[:, :, None]), 0.0)
    row_total = jnp.sum(weights, axis=2)
    update = jnp.einsum(
        "qhk,khd->qhd", weights.astype(jnp.bfloat16), v_three, preferred_element_type=jnp.float32
    )
    row_accum = update
    return (new_max, row_total, row_accum)


def local(
    residual, queries, keys, values, w_out, moe_gain, expert_ids, gate_weights, w_gate, w_up, w_down
):
    block_rows, col_width = queries.shape
    head_dim = D // H
    heads_here = col_width // head_dim
    experts_here = w_gate.shape[0]
    columns = lax.axis_size("ctx")
    ctx_index = lax.axis_index("ctx")
    query_pos = ctx_index * block_rows + jnp.arange(block_rows, dtype=jnp.int32)
    q_three = queries.reshape(block_rows, heads_here, head_dim)
    start_state = (
        jnp.full((block_rows, heads_here), -1e30, jnp.float32),
        jnp.zeros((block_rows, heads_here), jnp.float32),
        jnp.zeros((block_rows, heads_here, head_dim), jnp.float32),
    )
    row_max, row_total, row_accum = attend(
        start_state,
        gather_keys_values(keys, values, columns),
        q_three,
        query_pos,
    )
    attn_heads = (
        (row_accum / row_total[:, :, None]).reshape(block_rows, col_width).astype(jnp.bfloat16)
    )
    routing = lax.all_gather(
        jnp.concatenate([expert_ids.astype(jnp.float32), gate_weights], axis=1),
        "ctx",
        axis=0,
        tiled=True,
    )
    here = (ctx_index * experts_here + jnp.arange(experts_here, dtype=jnp.int32)).astype(
        jnp.float32
    )
    match = routing[:, :K, None] == here[None, None, :]
    chosen = jnp.any(match, axis=1)
    gates = jnp.sum(jnp.where(match, routing[:, K:, None], 0.0), axis=1)
    before = jnp.tril(jnp.ones((block_rows, block_rows), jnp.bfloat16), -1)
    rank = jnp.einsum(
        "ut,btj->buj",
        before,
        chosen.astype(jnp.bfloat16).reshape(columns, block_rows, experts_here),
        preferred_element_type=jnp.float32,
    )
    groups = columns // GROUP
    offset = ((jnp.arange(columns) % GROUP) * CAP).astype(jnp.float32)[:, None, None]
    place = jnp.where(
        chosen.reshape(columns, block_rows, experts_here), rank + offset, -1.0
    ).reshape(groups, GROUP * block_rows, experts_here)
    slots = jnp.arange(GROUP * CAP, dtype=jnp.int32).astype(jnp.float32)
    place_t = place.transpose(0, 2, 1)
    pick = place_t[:, :, None, :] == slots[None, None, :, None]
    gates_t = gates.reshape(groups, GROUP * block_rows, experts_here).transpose(0, 2, 1)
    slot_gate = jnp.sum(jnp.where(pick, gates_t[:, :, None, :], 0.0), axis=3)
    pick = pick.astype(jnp.bfloat16)
    attn_cols = lax.psum_scatter(
        jnp.dot(attn_heads, w_out, preferred_element_type=jnp.float32).astype(jnp.bfloat16),
        "exp",
        scatter_dimension=1,
        tiled=True,
    ).astype(jnp.float32)
    post_cols = (residual.astype(jnp.float32) + attn_cols).astype(jnp.bfloat16)
    post_wide = lax.all_gather(post_cols, "exp", axis=1, tiled=True).astype(jnp.float32)
    mean_square = jnp.mean(post_wide * post_wide, axis=1, keepdims=True)
    moe_rows = (post_wide * lax.rsqrt(mean_square + epsilon) * moe_gain[None, :]).astype(
        jnp.bfloat16
    )
    moe_all = lax.all_gather(moe_rows, "ctx", axis=0, tiled=True)
    packed = jnp.einsum(
        "gjst,gtd->gjsd",
        pick,
        moe_all.reshape(groups, GROUP * block_rows, D),
        preferred_element_type=jnp.float32,
    ).astype(jnp.bfloat16)
    gate_column = slot_gate.transpose(1, 0, 2).reshape(experts_here, groups * GROUP * CAP, 1)
    expert_out = run_experts(packed, gate_column, w_gate, w_up, w_down, lax.axis_size("exp"))
    partial = jnp.einsum("gjst,gjsd->gtd", pick, expert_out, preferred_element_type=jnp.float32)
    combined = scatter_sum(
        partial.astype(jnp.bfloat16).reshape(columns, block_rows, col_width), columns
    )
    return (post_cols.astype(jnp.float32) + combined).astype(jnp.bfloat16)


def solution(mesh):
    placed = (
        P("ctx", "exp"),
        P("ctx", "exp"),
        P("ctx", "exp"),
        P("ctx", "exp"),
        P("exp", None),
        P(),
        P("ctx", None),
        P("ctx", None),
        P("ctx", None, "exp"),
        P("ctx", None, "exp"),
        P("ctx", None, "exp"),
    )
    return jax.shard_map(
        local, mesh=mesh, in_specs=placed, out_specs=P("ctx", "exp"), check_vma=False
    )
```

```python
import functools
import math

import jax
import jax.numpy as jnp
from jax import lax
from jax.experimental import pallas as pl
from jax.experimental.pallas import tpu as pltpu
from jax.sharding import PartitionSpec as P

D = 2048
H = 16
K = 8
CAP = 36
GROUP = 4
LAG = 2
MESH = pl.DeviceIdType.MESH


epsilon = 1e-05


def gather_kernel(
    n,
    k_ref,
    v_ref,
    r_ref,
    ko_ref,
    vo_ref,
    ro_ref,
    own_sem,
    far_send,
    far_recv,
    sib_send,
    sib_recv,
):
    me = lax.axis_index("ctx")
    core, chip, chips = lax.rem(me, 2), me // 2, n // 2
    rows = k_ref.shape[0]
    sibling = chip * 2 + 1 - core
    peers = [lax.rem(chip + d, chips) * 2 + core for d in range(1, chips)]
    barrier = pltpu.get_barrier_semaphore()
    for other in [sibling] + peers:
        pl.semaphore_signal(barrier, inc=1, device_id={"ctx": other}, device_id_type=MESH)
    pl.semaphore_wait(barrier, chips)

    def block(ref, index):
        return ref.at[pl.ds(pl.multiple_of(index * rows, rows), rows)]

    pairs = ((k_ref, ko_ref), (v_ref, vo_ref), (r_ref, ro_ref))
    far, near, own = [], [], []
    for a, (src, dst) in enumerate(pairs):
        for d, peer in enumerate(peers):
            copy = pltpu.make_async_remote_copy(
                src_ref=src,
                dst_ref=block(dst, me),
                send_sem=far_send.at[a, d],
                recv_sem=far_recv.at[a, d],
                device_id={"ctx": peer},
                device_id_type=MESH,
            )
            copy.start()
            far.append((a, d, copy))
    for a, (src, dst) in enumerate(pairs):
        copy = pltpu.make_async_remote_copy(
            src_ref=src,
            dst_ref=block(dst, me),
            send_sem=sib_send.at[a, chips - 1],
            recv_sem=sib_recv.at[a, chips - 1],
            device_id={"ctx": sibling},
            device_id_type=MESH,
        )
        copy.start()
        near.append(copy)
        copy = pltpu.make_async_copy(src, block(dst, me), own_sem.at[a])
        copy.start()
        own.append(copy)
    for a, d, copy in far:
        copy.wait_recv()
        origin = lax.rem(chip + chips - d - 1, chips) * 2 + core
        dst = pairs[a][1]
        onward = pltpu.make_async_remote_copy(
            src_ref=block(dst, origin),
            dst_ref=block(dst, origin),
            send_sem=sib_send.at[a, d],
            recv_sem=sib_recv.at[a, d],
            device_id={"ctx": sibling},
            device_id_type=MESH,
        )
        onward.start()
        near.append(onward)
    for copy in own:
        copy.wait()
    for _, _, copy in far:
        copy.wait_send()
    for copy in near:
        copy.wait()


def gather_blocks(arrays, n):
    return pl.pallas_call(
        functools.partial(gather_kernel, n),
        out_shape=[jax.ShapeDtypeStruct((n * a.shape[0], a.shape[1]), a.dtype) for a in arrays],
        in_specs=[pl.BlockSpec(memory_space=pl.ANY)] * 3,
        out_specs=[pl.BlockSpec(memory_space=pl.ANY)] * 3,
        scratch_shapes=[
            pltpu.SemaphoreType.DMA((3,)),
            pltpu.SemaphoreType.DMA((3, n // 2)),
            pltpu.SemaphoreType.DMA((3, n // 2)),
            pltpu.SemaphoreType.DMA((3, n // 2)),
            pltpu.SemaphoreType.DMA((3, n // 2)),
        ],
        compiler_params=pltpu.CompilerParams(collective_id=1, has_side_effects=True),
        cost_estimate=pl.CostEstimate(flops=0, bytes_accessed=60_000_000, transcendentals=0),
    )(*arrays)


def expert_kernel(n, count, pick_ref, all_ref, g_ref, wg_ref, wu_ref, wd_ref, out_ref, held, send, recv):
    me = lax.axis_index("exp")
    step = pl.program_id(0)
    groups, _, slots, _ = pick_ref.shape
    rows = groups * slots
    units = wg_ref.shape[2]
    has_left, has_right = me > 0, me < n - 1

    def hop(side, source, expert):
        return pltpu.make_async_remote_copy(
            src_ref=held.at[source, expert],
            dst_ref=held.at[source, expert],
            send_sem=send.at[side, source, expert],
            recv_sem=recv.at[source, expert],
            device_id={"exp": me + 1 if side else me - 1},
            device_id_type=MESH,
        )

    barrier = pltpu.get_barrier_semaphore()

    @pl.when(step == 0)
    def _():
        for side, there in ((0, has_left), (1, has_right)):

            @pl.when(there)
            def _():
                pl.semaphore_signal(
                    barrier,
                    inc=1,
                    device_id={"exp": me + 1 if side else me - 1},
                    device_id_type=MESH,
                )

        pl.semaphore_wait(barrier, jnp.minimum(me, 1) + jnp.minimum(n - 1 - me, 1))

    @pl.when(step < count)
    def _():
        x = jnp.concatenate(
            [
                jnp.dot(pick_ref[g, 0], all_ref[g], preferred_element_type=jnp.float32).astype(
                    jnp.bfloat16
                )
                for g in range(groups)
            ],
            axis=0,
        )
        gate = jnp.dot(x, wg_ref[0], preferred_element_type=jnp.float32)
        up = jnp.dot(x, wu_ref[0], preferred_element_type=jnp.float32)
        hidden = gate / (1.0 + jnp.exp(-gate)) * up * g_ref[0]
        held[me, step] = hidden.astype(jnp.bfloat16)
        for side, there in ((0, has_left), (1, has_right)):

            @pl.when(there)
            def _():
                hop(side, me, step).start()

    for distance in range(1, n):
        expert = step - LAG * distance
        for side in (0, 1):
            source = me + distance if side == 0 else me - distance
            onward = has_left if side == 0 else has_right
            inside = (source < n) if side == 0 else (source >= 0)

            @pl.when((expert >= 0) & (expert < count) & inside)
            def _():
                hop(side, source, expert).wait_recv()

                @pl.when(onward)
                def _():
                    hop(side, source, expert).start()

    done = step - LAG * (n - 1)

    @pl.when(done >= 0)
    def _():
        total = jnp.zeros((rows, wd_ref.shape[2]), jnp.float32)
        for source in range(n):
            total += jnp.dot(
                held[source, done],
                wd_ref[0, source * units : (source + 1) * units],
                preferred_element_type=jnp.float32,
            )
        out_ref[...] = total.astype(jnp.bfloat16).reshape(out_ref.shape)

    @pl.when(done == count - 1)
    def _():
        for source in range(n):
            for side, there in (
                (0, has_left & (me <= source)),
                (1, has_right & (me >= source)),
            ):

                @pl.when(there)
                def _():
                    @pl.loop(0, count)
                    def _(expert):
                        hop(side, source, expert).wait_send()


def run_experts(pick, moe_all, slot_gate, w_gate, w_up, w_down, n):
    groups, count, slots, tokens = pick.shape
    width = moe_all.shape[2]
    rows = groups * slots
    units, hidden, columns = w_gate.shape[2], w_down.shape[1], w_down.shape[2]
    late = LAG * (n - 1)

    def first(step):
        return jnp.minimum(step, count - 1)

    def second(step):
        return jnp.maximum(step - late, 0)

    return pl.pallas_call(
        functools.partial(expert_kernel, n, count),
        grid=(count + late,),
        out_shape=jax.ShapeDtypeStruct((groups, count, slots, columns), jnp.bfloat16),
        in_specs=[
            pl.BlockSpec((groups, 1, slots, tokens), lambda i: (0, first(i), 0, 0)),
            pl.BlockSpec(
                (groups, tokens, width), lambda i: (0, 0, 0), pipeline_mode=pl.Buffered(1)
            ),
            pl.BlockSpec((1, rows, 1), lambda i: (first(i), 0, 0)),
            pl.BlockSpec((1, width, units), lambda i: (first(i), 0, 0)),
            pl.BlockSpec((1, width, units), lambda i: (first(i), 0, 0)),
            pl.BlockSpec((1, hidden, columns), lambda i: (second(i), 0, 0)),
        ],
        out_specs=pl.BlockSpec((groups, 1, slots, columns), lambda i: (0, second(i), 0, 0)),
        scratch_shapes=[
            pltpu.VMEM((n, count, rows, units), jnp.bfloat16),
            pltpu.SemaphoreType.DMA((2, n, count)),
            pltpu.SemaphoreType.DMA((n, count)),
        ],
        compiler_params=pltpu.CompilerParams(
            collective_id=2, has_side_effects=True, vmem_limit_bytes=56 * 1024 * 1024
        ),
        cost_estimate=pl.CostEstimate(
            flops=8_000_000_000, bytes_accessed=100_000_000, transcendentals=0
        ),
    )(pick, moe_all, slot_gate, w_gate, w_up, w_down)


def scatter_kernel(n, part_ref, out_ref, near, stage, far, near_send, near_recv, send, recv):
    me = lax.axis_index("ctx")
    core, chip, chips = lax.rem(me, 2), me // 2, n // 2
    sibling = chip * 2 + 1 - core
    barrier = pltpu.get_barrier_semaphore()
    for other in [sibling] + [lax.rem(chip + d, chips) * 2 + core for d in range(1, chips)]:
        pl.semaphore_signal(barrier, inc=1, device_id={"ctx": other}, device_id_type=MESH)
    pl.semaphore_wait(barrier, chips)

    def pass_over(d):
        target = lax.rem(chip + d, chips)
        return pltpu.make_async_remote_copy(
            src_ref=part_ref.at[target * 2 + 1 - core],
            dst_ref=near.at[d],
            send_sem=near_send.at[d],
            recv_sem=near_recv.at[d],
            device_id={"ctx": sibling},
            device_id_type=MESH,
        )

    def send_off(d):
        return pltpu.make_async_remote_copy(
            src_ref=stage.at[d],
            dst_ref=far.at[d],
            send_sem=send.at[d],
            recv_sem=recv.at[d],
            device_id={"ctx": lax.rem(chip + d, chips) * 2 + core},
            device_id_type=MESH,
        )

    order = list(range(1, chips)) + [0]
    for d in order:
        pass_over(d).start()
    for d in order:
        pass_over(d).wait_recv()
        mine = part_ref[lax.rem(chip + d, chips) * 2 + core].astype(jnp.float32)
        both = mine + near[d].astype(jnp.float32)
        if d:
            stage[d] = both.astype(jnp.bfloat16)
            send_off(d).start()
        else:
            out_ref[...] = both
    for d in range(1, chips):
        send_off(d).wait_recv()
        out_ref[...] += far[d].astype(jnp.float32)
    for d in range(1, chips):
        send_off(d).wait_send()
    for d in order:
        pass_over(d).wait_send()


def scatter_sum(part, n):
    _, rows, width = part.shape
    half = pltpu.VMEM((n // 2, rows, width), jnp.bfloat16)
    sems = pltpu.SemaphoreType.DMA((n // 2,))
    return pl.pallas_call(
        functools.partial(scatter_kernel, n),
        out_shape=jax.ShapeDtypeStruct((rows, width), jnp.float32),
        in_specs=[pl.BlockSpec(memory_space=pltpu.VMEM)],
        out_specs=pl.BlockSpec(memory_space=pltpu.VMEM),
        scratch_shapes=[half, half, half, sems, sems, sems, sems],
        compiler_params=pltpu.CompilerParams(
            collective_id=3, has_side_effects=True, vmem_limit_bytes=40 * 1024 * 1024
        ),
    )(part)


def attend(carried, pieces, q_three, query_pos):
    row_max, row_total, row_accum = carried
    key_piece, value_piece = pieces
    piece_rows = key_piece.shape[0]
    heads_here = q_three.shape[1]
    head_dim = q_three.shape[2]
    k_three = key_piece.reshape(piece_rows, heads_here, head_dim)
    v_three = value_piece.reshape(piece_rows, heads_here, head_dim)
    score_scale = 1.0 / math.sqrt(head_dim)
    scores = (
        jnp.einsum("qhd,khd->qhk", q_three, k_three, preferred_element_type=jnp.float32)
        * score_scale
    )
    allowed = (jnp.arange(piece_rows, dtype=jnp.int32)[None, :] <= query_pos[:, None])[:, None, :]
    masked = jnp.where(allowed, scores, -1e30)
    new_max = jnp.maximum(row_max, jnp.max(masked, axis=2))
    weights = jnp.where(allowed, jnp.exp(masked - new_max[:, :, None]), 0.0)
    row_total = jnp.sum(weights, axis=2)
    update = jnp.einsum(
        "qhk,khd->qhd", weights.astype(jnp.bfloat16), v_three, preferred_element_type=jnp.float32
    )
    row_accum = update
    return (new_max, row_total, row_accum)


def local(
    residual, queries, keys, values, w_out, moe_gain, expert_ids, gate_weights, w_gate, w_up, w_down
):
    block_rows, col_width = queries.shape
    head_dim = D // H
    heads_here = col_width // head_dim
    experts_here = w_gate.shape[0]
    columns = lax.axis_size("ctx")
    ctx_index = lax.axis_index("ctx")
    query_pos = ctx_index * block_rows + jnp.arange(block_rows, dtype=jnp.int32)
    q_three = queries.reshape(block_rows, heads_here, head_dim)
    start_state = (
        jnp.full((block_rows, heads_here), -1e30, jnp.float32),
        jnp.zeros((block_rows, heads_here), jnp.float32),
        jnp.zeros((block_rows, heads_here, head_dim), jnp.float32),
    )
    keys_all, values_all, routing = gather_blocks(
        (keys, values, jnp.concatenate([expert_ids.astype(jnp.float32), gate_weights], axis=1)),
        columns,
    )
    row_max, row_total, row_accum = attend(
        start_state,
        (keys_all, values_all),
        q_three,
        query_pos,
    )
    attn_heads = (
        (row_accum / row_total[:, :, None]).reshape(block_rows, col_width).astype(jnp.bfloat16)
    )
    here = (ctx_index * experts_here + jnp.arange(experts_here, dtype=jnp.int32)).astype(
        jnp.float32
    )
    match = routing[:, :K, None] == here[None, None, :]
    chosen = jnp.any(match, axis=1)
    gates = jnp.sum(jnp.where(match, routing[:, K:, None], 0.0), axis=1)
    before = jnp.tril(jnp.ones((block_rows, block_rows), jnp.bfloat16), -1)
    rank = jnp.einsum(
        "ut,btj->buj",
        before,
        chosen.astype(jnp.bfloat16).reshape(columns, block_rows, experts_here),
        preferred_element_type=jnp.float32,
    )
    groups = columns // GROUP
    offset = ((jnp.arange(columns) % GROUP) * CAP).astype(jnp.float32)[:, None, None]
    place = jnp.where(
        chosen.reshape(columns, block_rows, experts_here), rank + offset, -1.0
    ).reshape(groups, GROUP * block_rows, experts_here)
    slots = jnp.arange(GROUP * CAP, dtype=jnp.int32).astype(jnp.float32)
    place_t = place.transpose(0, 2, 1)
    pick = place_t[:, :, None, :] == slots[None, None, :, None]
    gates_t = gates.reshape(groups, GROUP * block_rows, experts_here).transpose(0, 2, 1)
    slot_gate = jnp.sum(jnp.where(pick, gates_t[:, :, None, :], 0.0), axis=3)
    pick = pick.astype(jnp.bfloat16)
    attn_cols = lax.psum_scatter(
        jnp.dot(attn_heads, w_out, preferred_element_type=jnp.float32).astype(jnp.bfloat16),
        "exp",
        scatter_dimension=1,
        tiled=True,
    ).astype(jnp.float32)
    post_cols = (residual.astype(jnp.float32) + attn_cols).astype(jnp.bfloat16)
    post_wide = lax.all_gather(post_cols, "exp", axis=1, tiled=True).astype(jnp.float32)
    mean_square = jnp.mean(post_wide * post_wide, axis=1, keepdims=True)
    moe_rows = (post_wide * lax.rsqrt(mean_square + epsilon) * moe_gain[None, :]).astype(
        jnp.bfloat16
    )
    moe_all = lax.all_gather(moe_rows, "ctx", axis=0, tiled=True)
    gate_column = slot_gate.transpose(1, 0, 2).reshape(experts_here, groups * GROUP * CAP, 1)
    expert_out = run_experts(
        pick,
        moe_all.reshape(groups, GROUP * block_rows, D),
        gate_column,
        w_gate,
        w_up,
        w_down,
        lax.axis_size("exp"),
    )
    partial = jnp.einsum("gjst,gjsd->gtd", pick, expert_out, preferred_element_type=jnp.float32)
    combined = scatter_sum(
        partial.astype(jnp.bfloat16).reshape(columns, block_rows, col_width), columns
    )
    return (post_cols.astype(jnp.float32) + combined).astype(jnp.bfloat16)


def solution(mesh):
    placed = (
        P("ctx", "exp"),
        P("ctx", "exp"),
        P("ctx", "exp"),
        P("ctx", "exp"),
        P("exp", None),
        P(),
        P("ctx", None),
        P("ctx", None),
        P("ctx", None, "exp"),
        P("ctx", None, "exp"),
        P("ctx", None, "exp"),
    )
    return jax.shard_map(
        local, mesh=mesh, in_specs=placed, out_specs=P("ctx", "exp"), check_vma=False
    )
```

```python
import functools
import math

import jax
import jax.numpy as jnp
from jax import lax
from jax.experimental import pallas as pl
from jax.experimental.pallas import tpu as pltpu
from jax.sharding import PartitionSpec as P

D = 2048
H = 16
K = 8
CAP = 36
GROUP = 4
LAG = 2
MESH = pl.DeviceIdType.MESH


epsilon = 1e-05


def gather_kernel(
    n,
    k_ref,
    v_ref,
    r_ref,
    ko_ref,
    vo_ref,
    ro_ref,
    own_sem,
    far_send,
    far_recv,
    sib_send,
    sib_recv,
):
    me = lax.axis_index("ctx")
    core, chip, chips = lax.rem(me, 2), me // 2, n // 2
    rows = k_ref.shape[0]
    sibling = chip * 2 + 1 - core
    peers = [lax.rem(chip + d, chips) * 2 + core for d in range(1, chips)]
    barrier = pltpu.get_barrier_semaphore()
    for other in [sibling] + peers:
        pl.semaphore_signal(barrier, inc=1, device_id={"ctx": other}, device_id_type=MESH)
    pl.semaphore_wait(barrier, chips)

    def block(ref, index):
        return ref.at[pl.ds(pl.multiple_of(index * rows, rows), rows)]

    pairs = ((k_ref, ko_ref), (v_ref, vo_ref), (r_ref, ro_ref))
    far, near, own = [], [], []
    for a, (src, dst) in enumerate(pairs):
        for d, peer in enumerate(peers):
            copy = pltpu.make_async_remote_copy(
                src_ref=src,
                dst_ref=block(dst, me),
                send_sem=far_send.at[a, d],
                recv_sem=far_recv.at[a, d],
                device_id={"ctx": peer},
                device_id_type=MESH,
            )
            copy.start()
            far.append((a, d, copy))
    for a, (src, dst) in enumerate(pairs):
        copy = pltpu.make_async_remote_copy(
            src_ref=src,
            dst_ref=block(dst, me),
            send_sem=sib_send.at[a, chips - 1],
            recv_sem=sib_recv.at[a, chips - 1],
            device_id={"ctx": sibling},
            device_id_type=MESH,
        )
        copy.start()
        near.append(copy)
        copy = pltpu.make_async_copy(src, block(dst, me), own_sem.at[a])
        copy.start()
        own.append(copy)
    for a, d, copy in far:
        copy.wait_recv()
        origin = lax.rem(chip + chips - d - 1, chips) * 2 + core
        dst = pairs[a][1]
        onward = pltpu.make_async_remote_copy(
            src_ref=block(dst, origin),
            dst_ref=block(dst, origin),
            send_sem=sib_send.at[a, d],
            recv_sem=sib_recv.at[a, d],
            device_id={"ctx": sibling},
            device_id_type=MESH,
        )
        onward.start()
        near.append(onward)
    for copy in own:
        copy.wait()
    for _, _, copy in far:
        copy.wait_send()
    for copy in near:
        copy.wait()


def gather_blocks(arrays, n):
    return pl.pallas_call(
        functools.partial(gather_kernel, n),
        out_shape=[jax.ShapeDtypeStruct((n * a.shape[0], a.shape[1]), a.dtype) for a in arrays],
        in_specs=[pl.BlockSpec(memory_space=pl.ANY)] * 3,
        out_specs=[pl.BlockSpec(memory_space=pl.ANY)] * 3,
        scratch_shapes=[
            pltpu.SemaphoreType.DMA((3,)),
            pltpu.SemaphoreType.DMA((3, n // 2)),
            pltpu.SemaphoreType.DMA((3, n // 2)),
            pltpu.SemaphoreType.DMA((3, n // 2)),
            pltpu.SemaphoreType.DMA((3, n // 2)),
        ],
        compiler_params=pltpu.CompilerParams(collective_id=1, has_side_effects=True),
        cost_estimate=pl.CostEstimate(flops=0, bytes_accessed=60_000_000, transcendentals=0),
    )(*arrays)


def expert_kernel(n, count, pick_ref, all_ref, g_ref, wg_ref, wu_ref, wd_ref, out_ref, held, send, recv):
    me = lax.axis_index("exp")
    step = pl.program_id(0)
    groups, _, slots, _ = pick_ref.shape
    rows = groups * slots
    units = wg_ref.shape[2]
    has_left, has_right = me > 0, me < n - 1

    def hop(side, source, expert):
        return pltpu.make_async_remote_copy(
            src_ref=held.at[source, expert],
            dst_ref=held.at[source, expert],
            send_sem=send.at[side, source, expert],
            recv_sem=recv.at[source, expert],
            device_id={"exp": me + 1 if side else me - 1},
            device_id_type=MESH,
        )

    barrier = pltpu.get_barrier_semaphore()

    @pl.when(step == 0)
    def _():
        for side, there in ((0, has_left), (1, has_right)):

            @pl.when(there)
            def _():
                pl.semaphore_signal(
                    barrier,
                    inc=1,
                    device_id={"exp": me + 1 if side else me - 1},
                    device_id_type=MESH,
                )

        pl.semaphore_wait(barrier, jnp.minimum(me, 1) + jnp.minimum(n - 1 - me, 1))

    @pl.when(step < count)
    def _():
        x = jnp.concatenate(
            [
                jnp.dot(pick_ref[g, 0], all_ref[g], preferred_element_type=jnp.float32).astype(
                    jnp.bfloat16
                )
                for g in range(groups)
            ],
            axis=0,
        )
        gate = jnp.dot(x, wg_ref[0], preferred_element_type=jnp.float32)
        up = jnp.dot(x, wu_ref[0], preferred_element_type=jnp.float32)
        hidden = gate / (1.0 + jnp.exp(-gate)) * up * g_ref[0]
        held[me, step] = hidden.astype(jnp.bfloat16)
        for side, there in ((0, has_left), (1, has_right)):

            @pl.when(there)
            def _():
                hop(side, me, step).start()

    for distance in range(1, n):
        expert = step - LAG * distance
        for side in (0, 1):
            source = me + distance if side == 0 else me - distance
            onward = has_left if side == 0 else has_right
            inside = (source < n) if side == 0 else (source >= 0)

            @pl.when((expert >= 0) & (expert < count) & inside)
            def _():
                hop(side, source, expert).wait_recv()

                @pl.when(onward)
                def _():
                    hop(side, source, expert).start()

    done = step - LAG * (n - 1)

    @pl.when(done >= 0)
    def _():
        total = jnp.zeros((rows, wd_ref.shape[2]), jnp.float32)
        for source in range(n):
            total += jnp.dot(
                held[source, done],
                wd_ref[0, source * units : (source + 1) * units],
                preferred_element_type=jnp.float32,
            )
        out_ref[...] = total.astype(jnp.bfloat16).reshape(out_ref.shape)

    @pl.when(done == count - 1)
    def _():
        for source in range(n):
            for side, there in (
                (0, has_left & (me <= source)),
                (1, has_right & (me >= source)),
            ):

                @pl.when(there)
                def _():
                    @pl.loop(0, count)
                    def _(expert):
                        hop(side, source, expert).wait_send()


def run_experts(pick, moe_all, slot_gate, w_gate, w_up, w_down, n):
    groups, count, slots, tokens = pick.shape
    width = moe_all.shape[2]
    rows = groups * slots
    units, hidden, columns = w_gate.shape[2], w_down.shape[1], w_down.shape[2]
    late = LAG * (n - 1)

    def first(step):
        return jnp.minimum(step, count - 1)

    def second(step):
        return jnp.maximum(step - late, 0)

    return pl.pallas_call(
        functools.partial(expert_kernel, n, count),
        grid=(count + late,),
        out_shape=jax.ShapeDtypeStruct((groups, count, slots, columns), jnp.bfloat16),
        in_specs=[
            pl.BlockSpec((groups, 1, slots, tokens), lambda i: (0, first(i), 0, 0)),
            pl.BlockSpec(
                (groups, tokens, width), lambda i: (0, 0, 0), pipeline_mode=pl.Buffered(1)
            ),
            pl.BlockSpec((1, rows, 1), lambda i: (first(i), 0, 0)),
            pl.BlockSpec((1, width, units), lambda i: (first(i), 0, 0)),
            pl.BlockSpec((1, width, units), lambda i: (first(i), 0, 0)),
            pl.BlockSpec((1, hidden, columns), lambda i: (second(i), 0, 0)),
        ],
        out_specs=pl.BlockSpec((groups, 1, slots, columns), lambda i: (0, second(i), 0, 0)),
        scratch_shapes=[
            pltpu.VMEM((n, count, rows, units), jnp.bfloat16),
            pltpu.SemaphoreType.DMA((2, n, count)),
            pltpu.SemaphoreType.DMA((n, count)),
        ],
        compiler_params=pltpu.CompilerParams(
            collective_id=2, has_side_effects=True, vmem_limit_bytes=56 * 1024 * 1024
        ),
        cost_estimate=pl.CostEstimate(
            flops=8_000_000_000, bytes_accessed=100_000_000, transcendentals=0
        ),
    )(pick, moe_all, slot_gate, w_gate, w_up, w_down)


def scatter_kernel(n, part_ref, out_ref, near, stage, far, near_send, near_recv, send, recv):
    me = lax.axis_index("ctx")
    core, chip, chips = lax.rem(me, 2), me // 2, n // 2
    sibling = chip * 2 + 1 - core
    barrier = pltpu.get_barrier_semaphore()
    for other in [sibling] + [lax.rem(chip + d, chips) * 2 + core for d in range(1, chips)]:
        pl.semaphore_signal(barrier, inc=1, device_id={"ctx": other}, device_id_type=MESH)
    pl.semaphore_wait(barrier, chips)

    def pass_over(d):
        target = lax.rem(chip + d, chips)
        return pltpu.make_async_remote_copy(
            src_ref=part_ref.at[target * 2 + 1 - core],
            dst_ref=near.at[d],
            send_sem=near_send.at[d],
            recv_sem=near_recv.at[d],
            device_id={"ctx": sibling},
            device_id_type=MESH,
        )

    def send_off(d):
        return pltpu.make_async_remote_copy(
            src_ref=stage.at[d],
            dst_ref=far.at[d],
            send_sem=send.at[d],
            recv_sem=recv.at[d],
            device_id={"ctx": lax.rem(chip + d, chips) * 2 + core},
            device_id_type=MESH,
        )

    order = list(range(1, chips)) + [0]
    for d in order:
        pass_over(d).start()
    for d in order:
        pass_over(d).wait_recv()
        mine = part_ref[lax.rem(chip + d, chips) * 2 + core].astype(jnp.float32)
        both = mine + near[d].astype(jnp.float32)
        if d:
            stage[d] = both.astype(jnp.bfloat16)
            send_off(d).start()
        else:
            out_ref[...] = both
    for d in range(1, chips):
        send_off(d).wait_recv()
        out_ref[...] += far[d].astype(jnp.float32)
    for d in range(1, chips):
        send_off(d).wait_send()
    for d in order:
        pass_over(d).wait_send()


def scatter_sum(part, n):
    _, rows, width = part.shape
    half = pltpu.VMEM((n // 2, rows, width), jnp.bfloat16)
    sems = pltpu.SemaphoreType.DMA((n // 2,))
    return pl.pallas_call(
        functools.partial(scatter_kernel, n),
        out_shape=jax.ShapeDtypeStruct((rows, width), jnp.float32),
        in_specs=[pl.BlockSpec(memory_space=pltpu.VMEM)],
        out_specs=pl.BlockSpec(memory_space=pltpu.VMEM),
        scratch_shapes=[half, half, half, sems, sems, sems, sems],
        compiler_params=pltpu.CompilerParams(
            collective_id=3, has_side_effects=True, vmem_limit_bytes=40 * 1024 * 1024
        ),
    )(part)


def norm_kernel(
    n, part_ref, res_ref, gain_ref, rows_ref, post_ref, into, stage, wide, s_send, s_recv, send, recv
):
    me = lax.axis_index("exp")
    width = res_ref.shape[1]
    has_left, has_right = me > 0, me < n - 1
    barrier = pltpu.get_barrier_semaphore()
    for side, there in ((0, has_left), (1, has_right)):

        @pl.when(there)
        def _():
            pl.semaphore_signal(
                barrier,
                inc=1,
                device_id={"exp": me + 1 if side else me - 1},
                device_id_type=MESH,
            )

    pl.semaphore_wait(barrier, jnp.minimum(me, 1) + jnp.minimum(n - 1 - me, 1))

    def carry(side, target):
        return pltpu.make_async_remote_copy(
            src_ref=stage.at[target],
            dst_ref=into.at[side, target],
            send_sem=s_send.at[target],
            recv_sem=s_recv.at[side, target],
            device_id={"exp": me + 1 if side else me - 1},
            device_id_type=MESH,
        )

    def hop(side, source):
        return pltpu.make_async_remote_copy(
            src_ref=wide.at[source],
            dst_ref=wide.at[source],
            send_sem=send.at[side, source],
            recv_sem=recv.at[source],
            device_id={"exp": me + 1 if side else me - 1},
            device_id_type=MESH,
        )

    for i in range(n):
        for side, target in ((1, n - 1 - i), (0, i)):
            beyond = (target > me) if side else (target < me)
            feeder = has_left if side else has_right
            mine = part_ref.at[:, target * width : (target + 1) * width]

            @pl.when(beyond & feeder)
            def _():
                carry(side, target).wait_recv()
                total = mine[...].astype(jnp.float32) + into[side, target].astype(jnp.float32)
                stage[target] = total.astype(jnp.bfloat16)

            @pl.when(beyond & jnp.logical_not(feeder))
            def _():
                stage[target] = mine[...]

            @pl.when(beyond)
            def _():
                carry(side, target).start()

    for target in range(n):

        @pl.when(target == me)
        def _():
            mine = part_ref[:, target * width : (target + 1) * width]
            post_ref[...] = mine.astype(jnp.float32) + res_ref[...].astype(jnp.float32)
            for side, feeder in ((1, has_left), (0, has_right)):

                @pl.when(feeder)
                def _():
                    carry(side, target).wait_recv()
                    post_ref[...] += into[side, target].astype(jnp.float32)

    wide[me] = post_ref[...].astype(jnp.bfloat16)
    for side, there in ((0, has_left), (1, has_right)):

        @pl.when(there)
        def _():
            hop(side, me).start()

    for distance in range(1, n):
        for side in (0, 1):
            source = me + distance if side == 0 else me - distance
            onward = has_left if side == 0 else has_right
            inside = (source < n) if side == 0 else (source >= 0)

            @pl.when(inside)
            def _():
                hop(side, source).wait_recv()

                @pl.when(onward)
                def _():
                    hop(side, source).start()

    square_sum = jnp.zeros((res_ref.shape[0], 1), jnp.float32)
    for source in range(n):
        block = wide[source].astype(jnp.float32)
        square_sum += jnp.sum(block * block, axis=1, keepdims=True)
    scale = lax.rsqrt(square_sum / (n * width) + epsilon)
    for source in range(n):
        columns = slice(source * width, (source + 1) * width)
        block = wide[source].astype(jnp.float32)
        rows_ref[:, columns] = (block * scale * gain_ref[:, columns]).astype(jnp.bfloat16)
    for index in range(n):
        for side, there in ((0, has_left & (me <= index)), (1, has_right & (me >= index))):

            @pl.when(there)
            def _():
                hop(side, index).wait_send()

        for side, there in ((1, index > me), (0, index < me)):

            @pl.when(there)
            def _():
                carry(side, index).wait_send()


def sum_and_norm(part, residual, gain, n):
    rows, width = residual.shape
    return pl.pallas_call(
        functools.partial(norm_kernel, n),
        out_shape=(
            jax.ShapeDtypeStruct((rows, n * width), jnp.bfloat16),
            jax.ShapeDtypeStruct((rows, width), jnp.float32),
        ),
        in_specs=[pl.BlockSpec(memory_space=pltpu.VMEM)] * 3,
        out_specs=[pl.BlockSpec(memory_space=pltpu.VMEM)] * 2,
        scratch_shapes=[
            pltpu.VMEM((2, n, rows, width), jnp.bfloat16),
            pltpu.VMEM((n, rows, width), jnp.bfloat16),
            pltpu.VMEM((n, rows, width), jnp.bfloat16),
            pltpu.SemaphoreType.DMA((n,)),
            pltpu.SemaphoreType.DMA((2, n)),
            pltpu.SemaphoreType.DMA((2, n)),
            pltpu.SemaphoreType.DMA((n,)),
        ],
        compiler_params=pltpu.CompilerParams(
            collective_id=4, has_side_effects=True, vmem_limit_bytes=40 * 1024 * 1024
        ),
    )(part, residual, gain)


def attend(carried, pieces, q_three, query_pos):
    row_max, row_total, row_accum = carried
    key_piece, value_piece = pieces
    piece_rows = key_piece.shape[0]
    heads_here = q_three.shape[1]
    head_dim = q_three.shape[2]
    k_three = key_piece.reshape(piece_rows, heads_here, head_dim)
    v_three = value_piece.reshape(piece_rows, heads_here, head_dim)
    score_scale = 1.0 / math.sqrt(head_dim)
    scores = (
        jnp.einsum("qhd,khd->qhk", q_three, k_three, preferred_element_type=jnp.float32)
        * score_scale
    )
    allowed = (jnp.arange(piece_rows, dtype=jnp.int32)[None, :] <= query_pos[:, None])[:, None, :]
    masked = jnp.where(allowed, scores, -1e30)
    new_max = jnp.maximum(row_max, jnp.max(masked, axis=2))
    weights = jnp.where(allowed, jnp.exp(masked - new_max[:, :, None]), 0.0)
    row_total = jnp.sum(weights, axis=2)
    update = jnp.einsum(
        "qhk,khd->qhd", weights.astype(jnp.bfloat16), v_three, preferred_element_type=jnp.float32
    )
    row_accum = update
    return (new_max, row_total, row_accum)


def local(
    residual, queries, keys, values, w_out, moe_gain, expert_ids, gate_weights, w_gate, w_up, w_down
):
    block_rows, col_width = queries.shape
    head_dim = D // H
    heads_here = col_width // head_dim
    experts_here = w_gate.shape[0]
    columns = lax.axis_size("ctx")
    ctx_index = lax.axis_index("ctx")
    query_pos = ctx_index * block_rows + jnp.arange(block_rows, dtype=jnp.int32)
    q_three = queries.reshape(block_rows, heads_here, head_dim)
    start_state = (
        jnp.full((block_rows, heads_here), -1e30, jnp.float32),
        jnp.zeros((block_rows, heads_here), jnp.float32),
        jnp.zeros((block_rows, heads_here, head_dim), jnp.float32),
    )
    keys_all, values_all, routing = gather_blocks(
        (keys, values, jnp.concatenate([expert_ids.astype(jnp.float32), gate_weights], axis=1)),
        columns,
    )
    row_max, row_total, row_accum = attend(
        start_state,
        (keys_all, values_all),
        q_three,
        query_pos,
    )
    attn_heads = (
        (row_accum / row_total[:, :, None]).reshape(block_rows, col_width).astype(jnp.bfloat16)
    )
    here = (ctx_index * experts_here + jnp.arange(experts_here, dtype=jnp.int32)).astype(
        jnp.float32
    )
    match = routing[:, :K, None] == here[None, None, :]
    chosen = jnp.any(match, axis=1)
    gates = jnp.sum(jnp.where(match, routing[:, K:, None], 0.0), axis=1)
    before = jnp.tril(jnp.ones((block_rows, block_rows), jnp.bfloat16), -1)
    rank = jnp.einsum(
        "ut,btj->buj",
        before,
        chosen.astype(jnp.bfloat16).reshape(columns, block_rows, experts_here),
        preferred_element_type=jnp.float32,
    )
    groups = columns // GROUP
    offset = ((jnp.arange(columns) % GROUP) * CAP).astype(jnp.float32)[:, None, None]
    place = jnp.where(
        chosen.reshape(columns, block_rows, experts_here), rank + offset, -1.0
    ).reshape(groups, GROUP * block_rows, experts_here)
    slots = jnp.arange(GROUP * CAP, dtype=jnp.int32).astype(jnp.float32)
    place_t = place.transpose(0, 2, 1)
    pick = place_t[:, :, None, :] == slots[None, None, :, None]
    gates_t = gates.reshape(groups, GROUP * block_rows, experts_here).transpose(0, 2, 1)
    slot_gate = jnp.sum(jnp.where(pick, gates_t[:, :, None, :], 0.0), axis=3)
    pick = pick.astype(jnp.bfloat16)
    moe_rows, post_sum = sum_and_norm(
        jnp.dot(attn_heads, w_out, preferred_element_type=jnp.float32).astype(jnp.bfloat16),
        residual,
        moe_gain[None, :],
        lax.axis_size("exp"),
    )
    post_cols = post_sum.astype(jnp.bfloat16)
    moe_all = lax.all_gather(moe_rows, "ctx", axis=0, tiled=True)
    gate_column = slot_gate.transpose(1, 0, 2).reshape(experts_here, groups * GROUP * CAP, 1)
    expert_out = run_experts(
        pick,
        moe_all.reshape(groups, GROUP * block_rows, D),
        gate_column,
        w_gate,
        w_up,
        w_down,
        lax.axis_size("exp"),
    )
    partial = jnp.einsum("gjst,gjsd->gtd", pick, expert_out, preferred_element_type=jnp.float32)
    combined = scatter_sum(
        partial.astype(jnp.bfloat16).reshape(columns, block_rows, col_width), columns
    )
    return (post_cols.astype(jnp.float32) + combined).astype(jnp.bfloat16)


def solution(mesh):
    placed = (
        P("ctx", "exp"),
        P("ctx", "exp"),
        P("ctx", "exp"),
        P("ctx", "exp"),
        P("exp", None),
        P(),
        P("ctx", None),
        P("ctx", None),
        P("ctx", None, "exp"),
        P("ctx", None, "exp"),
        P("ctx", None, "exp"),
    )
    return jax.shard_map(
        local, mesh=mesh, in_specs=placed, out_specs=P("ctx", "exp"), check_vma=False
    )
```
